256 devices in a mesh: row: 16 (over x_hi, z), col: 16 (over y, x_lo, core).
Axes of the slice: x: 4 (x_hi: 2, x_lo: 2; x = x_hi * 2 + x_lo), y: 4, z: 8, core: 2. Of those that a mesh axis runs over, the one named last changes fastest.
Arguments:
- left_old: bfloat16 [16384, 16384], P('row', 'col'), may hold values from -6 to 6
- right_old: bfloat16 [16384, 16384], P('col', 'row'), may hold values from -6 to 6
- left_map: int32 [32, 32], P('row', 'col'), may hold values 0 or 1
- right_map: int32 [32, 32], P('col', 'row'), may hold values 0 or 1
- poles: float32 [16384], replicated, may hold values from 0.7 to 16385.3, as said below
- zvec: float32 [16384], replicated, may hold values from -6 to 6
- perm: int32 [16384], replicated, may hold values from 0 to 16383, each once
- gaps: float32 [2048], replicated, may hold values from 0.2 to 0.4
- root_pole: int32 [2048], replicated, may hold values from 0 to 12286, as said below
Outputs:
- left_new: bfloat16 [16384, 2048], P('row', 'col')
- right_new: bfloat16 [16384, 2048], P('col', 'row')
The draws below stay inside these ranges and needn't reach their ends.
Inputs may be any that keep to these rules, and one draw needn't show every extreme that they name: `perm`: each of 0 to 16383 once; indices from 12288 on are deflated. `root_pole`: distinct; root j lies between poles root_pole[j] and root_pole[j] + 1, both live. `poles`: Increasing, neighbours 0.6 or more apart.
All inputs are finite; a program needn't handle non-finite values. No bound on the sum of `left_map` or of `right_map` on one device may be relied on, other than what follows from the above.
Results may differ from the reference program's by a relative error of at most 0.02.
Values may be sent and summed in bfloat16 or wider, within the bound.
No kernel may reach another device: no remote copies, remote signals or barrier semaphores. Data moves between devices by JAX's collectives and lax.ppermute only.
A program may use at most 128 MiB of HBM per device.

```python
import jax
import jax.numpy as jnp
from jax import lax

N = 16384
M = 2048
TB = 512
LIVE = 12288
N_ROW = 16
N_COL = 16


def draw_poles(key, part):
    key = jax.random.fold_in(key, 11)
    spread = 0.1
    jitter = jax.random.uniform(key, (N,), jnp.float32, -spread, spread)
    return 1.0 + jnp.arange(N, dtype=jnp.float32) + jitter


def draw_root_pole(key, part):
    key = jax.random.fold_in(key, 12)
    return jax.random.permutation(key, LIVE - 1)[:M].astype(jnp.int32)


def plant(entries, rng, smallest, top_value):
    extent = entries.shape
    index_at = [jax.random.randint(jax.random.fold_in(rng, axis), (), 0, extent[axis]) for axis in range(len(extent))]
    entries = entries.at[tuple(index_at)].set(smallest)
    longest = extent.index(max(extent))
    index_at[longest] = (index_at[longest] + 1) % extent[longest]
    return entries.at[tuple(index_at)].set(top_value)


def block_scale(stream_key, extent, split, least, top_value):
    factor_of, own = 1.0, jax.random.fold_in(stream_key, 6)
    for position, blocks in split:
        draws = jnp.exp(jax.random.uniform(jax.random.fold_in(own, position), (blocks,), jnp.float32, least / len(split), top_value / len(split)))
        factor_of = factor_of * jnp.repeat(draws, extent[position] // blocks).reshape([-1 if axis == position else 1 for axis in range(len(extent))])
    return factor_of


def bell_draw(own_key, extent, deviation, bound, pieces=(), kind=jnp.bfloat16):
    array = deviation * jax.random.normal(own_key, extent, jnp.float32)
    if pieces:
        array = array * block_scale(own_key, extent, pieces, -0.22, 0.18)
    return jnp.clip(array, -bound, bound).astype(kind)


def setup_inputs(seed: int = 0) -> dict:
    key_list = jax.random.split(jax.random.key(seed), 10)
    return {
        "left_old": bell_draw(key_list[0], (N, N), 1.0, 6.0, ((0, 16), (1, 16))),
        "right_old": bell_draw(key_list[1], (N, N), 1.0, 6.0, ((0, 16), (1, 16))),
        "left_map": plant((jax.random.randint(key_list[2], (N // TB, N // TB), 0, 4) < 3).astype(jnp.int32), jax.random.fold_in(key_list[2], 1), 0, 1),
        "right_map": plant((jax.random.randint(key_list[3], (N // TB, N // TB), 0, 4) < 3).astype(jnp.int32), jax.random.fold_in(key_list[3], 1), 0, 1),
        "poles": draw_poles(jax.random.fold_in(key_list[9], 71), 0),
        "zvec": bell_draw(key_list[5], (N,), 1.0, 6.0, (), jnp.float32),
        "perm": jax.random.permutation(key_list[6], N).astype(jnp.int32),
        "gaps": jnp.clip(jax.random.uniform(key_list[7], (M,), jnp.float32, 0.2, 0.4), 0.2, 0.4),
        "root_pole": draw_root_pole(jax.random.fold_in(key_list[9], 71), 0),
    }


def combine(block, tiles, weights, width):
    count = tiles.shape[0]
    masked = (block.reshape(count, TB, count, TB) * tiles[:, None, :, None].astype(jnp.bfloat16)).reshape(N, N)
    total = jnp.zeros((N, weights.shape[1]), jnp.float32)
    for index in range(N // width):
        part = jnp.dot(masked[:, index * width:(index + 1) * width], weights[index * width:(index + 1) * width], preferred_element_type=jnp.float32)
        rounded = lax.optimization_barrier(part.astype(jnp.bfloat16))
        total = total + rounded.astype(jnp.float32)
    return total.astype(jnp.bfloat16)

def reference(left_old, right_old, left_map, right_map, poles, zvec, perm, gaps, root_pole):
    anchor = poles[root_pole]
    pole_sel = poles[perm]
    live = perm < LIVE
    live_z = jnp.where(live, zvec[perm], jnp.float32(0.0))
    diff = pole_sel[:, None] - anchor[None, :] - gaps[None, :]
    total = pole_sel[:, None] + anchor[None, :] + gaps[None, :]
    denom = diff * total
    left_w = live_z[:, None] / denom
    right_w = (live_z * pole_sel)[:, None] / denom
    left_n = (left_w / jnp.sqrt(lax.optimization_barrier(jnp.sum(left_w * left_w, axis=0)))[None, :]).astype(jnp.bfloat16)
    right_n = (right_w / jnp.sqrt(lax.optimization_barrier(jnp.sum(right_w * right_w, axis=0)))[None, :]).astype(jnp.bfloat16)
    left_new = combine(left_old, left_map, left_n, N // N_COL)
    right_new = combine(right_old, right_map, right_n, N // N_ROW)
    return (left_new, right_new)
```

```python
import functools

import jax
import jax.numpy as jnp
from jax import lax
from jax.experimental import pallas as pl
from jax.experimental.pallas import tpu as pltpu
from jax.sharding import PartitionSpec as P

N = 16384
M = 2048
TB = 512
LIVE = 12288
LANES = 128
BLOCK = 1024
X_ROWS = 512


def split3(x):
    hi = x.astype(jnp.bfloat16)
    rest = x - hi.astype(jnp.float32)
    mid = rest.astype(jnp.bfloat16)
    low = (rest - mid.astype(jnp.float32)).astype(jnp.bfloat16)
    return hi, mid, low


def lookup_kernel(rows_ref, perm_ref, poles_ref, zvec_ref, root_ref, gaps_ref, cols_ref, anchor_ref, table, rows):
    for index, ref in enumerate((poles_ref, zvec_ref)):
        for part, piece in enumerate(split3(jnp.transpose(ref[...]))):
            start = (3 * index + part) * LANES
            table[start : start + LANES, :] = piece
    sub = lax.broadcasted_iota(jnp.int32, (LANES, LANES), 0)

    def pick(index, with_z):
        high = index // LANES
        low = index - high * LANES
        onehot = (sub == high).astype(jnp.float32).astype(jnp.bfloat16)
        parts = table[...] if with_z else table[: 3 * LANES, :]
        got = jnp.dot(parts, onehot, preferred_element_type=jnp.float32)
        hit = sub == low

        def fold(base):
            whole = got[base : base + LANES] + got[base + LANES : base + 2 * LANES] + got[base + 2 * LANES : base + 3 * LANES]
            return jnp.sum(jnp.where(hit, whole, 0.0), axis=0, keepdims=True)

        return fold(0), (fold(3 * LANES) if with_z else None)

    rows[...] = jnp.zeros_like(rows)
    for side in range(2):
        for half in range(2):
            base = rows_ref[2 * side + half]
            for step in range(BLOCK // LANES):
                index = perm_ref[pl.ds(base + step, 1), :]
                pole, z = pick(index, True)
                z = jnp.where(index < LIVE, z, 0.0)
                at = slice(half * BLOCK + step * LANES, half * BLOCK + (step + 1) * LANES)
                rows[2 * side : 2 * side + 1, at] = pole
                rows[2 * side + 1 : 2 * side + 2, at] = z * pole if side else z
    cols_ref[...] = jnp.transpose(rows[...])
    for step in range(M // LANES):
        at = slice(step * LANES, (step + 1) * LANES)
        pole, _ = pick(root_ref[step : step + 1, :], False)
        gap = gaps_ref[step : step + 1, :]
        anchor_ref[0:1, at] = pole
        anchor_ref[1:2, at] = gap
        anchor_ref[2:3, at] = pole + gap


def lookup(starts, perm, poles, zvec, root_pole, gaps):
    whole = pl.BlockSpec(memory_space=pltpu.VMEM)
    return pl.pallas_call(
        lookup_kernel,
        out_shape=(
            jax.ShapeDtypeStruct((2 * BLOCK, 8), jnp.float32),
            jax.ShapeDtypeStruct((8, M), jnp.float32),
        ),
        in_specs=[pl.BlockSpec(memory_space=pltpu.SMEM)] + [whole] * 5,
        out_specs=(whole, whole),
        scratch_shapes=[
            pltpu.VMEM((6 * LANES, LANES), jnp.bfloat16),
            pltpu.VMEM((8, 2 * BLOCK), jnp.float32),
        ],
        cost_estimate=pl.CostEstimate(flops=10**9, bytes_accessed=2**20, transcendentals=0),
    )(
        starts,
        perm.reshape(LANES, LANES),
        poles.reshape(LANES, LANES),
        zvec.reshape(LANES, LANES),
        root_pole.reshape(M // LANES, LANES),
        gaps.reshape(M // LANES, LANES),
    )


def norm_kernel(poles_ref, zvec_ref, left_ref, right_ref, out_ref):
    def spread(ref, row):
        return jnp.transpose(jnp.broadcast_to(ref[row : row + 1, :], (LANES, LANES)))

    for side, ref in enumerate((left_ref, right_ref)):
        anchor, gap, both = spread(ref, 0), spread(ref, 1), spread(ref, 2)

        def step(row, total):
            pole = poles_ref[pl.ds(row, 1), :]
            z = zvec_ref[pl.ds(row, 1), :]
            if side:
                z = z * pole
            weight = z / (((pole - anchor) - gap) * (pole + both))
            return total + weight * weight

        total = lax.fori_loop(0, LIVE // LANES, step, jnp.zeros((LANES, LANES), jnp.float32))
        sums = jnp.sum(jnp.transpose(total), axis=0, keepdims=True)
        out_ref[side : side + 1, :] = 1.0 / jnp.sqrt(sums)


def norms(poles, zvec, left_anchor, right_anchor):
    whole = pl.BlockSpec(memory_space=pltpu.VMEM)
    return pl.pallas_call(
        norm_kernel,
        out_shape=jax.ShapeDtypeStruct((2, LANES), jnp.float32),
        in_specs=[whole] * 4,
        out_specs=whole,
        cost_estimate=pl.CostEstimate(flops=4 * 10**9, bytes_accessed=2**20, transcendentals=0),
    )(poles.reshape(LANES, LANES), zvec.reshape(LANES, LANES), left_anchor, right_anchor)


def apply_mask(block, tiles):
    row_tiles, col_tiles = tiles.shape
    shaped = block.reshape(row_tiles, TB, col_tiles, TB) * tiles[:, None, :, None].astype(
        jnp.bfloat16
    )
    return shaped.reshape(block.shape)


def weights(pole, z, anchor):
    diff = (pole - anchor[0:1]) - anchor[1:2]
    return (z / (diff * (pole + anchor[2:3]))).astype(jnp.bfloat16)


def dot(block, w):
    return jnp.dot(block, w, preferred_element_type=jnp.float32)


def z_step(value, shift):
    pairs = [(h * 8 + z, h * 8 + (z + shift) % 8) for h in range(2) for z in range(8)]
    return lax.ppermute(value, "row", pairs)


def x_hi_swap(value):
    return lax.ppermute(value, "row", [(r, (r + 8) % 16) for r in range(16)])


def y_step(value, shift):
    return lax.ppermute(value, "col", [(q, (q + 4 * shift) % 16) for q in range(16)])


def x_lo_swap(value):
    return lax.ppermute(value, "col", [(q, q ^ 2) for q in range(16)])


def core_swap(value):
    return lax.ppermute(value, "col", [(q, q ^ 1) for q in range(16)])


def ring(part, step, place, size):
    far = part((place + size // 2) % size).astype(jnp.bfloat16)
    half = far.shape[0] // 2
    up, down = step(far[:half], 1), step(far[half:], -1)
    for distance in range(size // 2 - 1, 0, -1):
        above = part((place + distance) % size)
        below = part((place - distance) % size)
        if up.shape[0] == half:
            above = jnp.concatenate([above[:half] + up.astype(jnp.float32), above[half:]])
            below = jnp.concatenate([below[:half], below[half:] + down.astype(jnp.float32)])
        else:
            above = above + up.astype(jnp.float32)
            below = below + down.astype(jnp.float32)
        up, down = step(above.astype(jnp.bfloat16), 1), step(below.astype(jnp.bfloat16), -1)
    return part(place) + up.astype(jnp.float32) + down.astype(jnp.float32)


def columns(anchor, shard):
    return lax.dynamic_slice_in_dim(anchor, shard * LANES, LANES, axis=1)


def body(left_old, right_old, left_map, right_map, poles, zvec, perm, gaps, root_pole):
    r, q = lax.axis_index("row"), lax.axis_index("col")
    h, z = r // 8, r % 8
    y, x, core = q // 4, (q // 2) % 2, q % 2
    per_block = BLOCK // LANES
    starts = jnp.stack([q * per_block, (q ^ 1) * per_block, r * per_block, ((r + 8) % 16) * per_block])
    cols, anchor = lookup(starts.astype(jnp.int32), perm, poles, zvec, root_pole, gaps)
    left_pole, left_z = cols[:, 0:1], cols[:, 1:2]
    right_pole, right_z = cols[:, 2:3], cols[:, 3:4]
    scale = norms(poles, zvec, columns(anchor, q), columns(anchor, r))

    right_ready = apply_mask(right_old, right_map)
    left_ready = apply_mask(left_old, left_map)
    z_rows = BLOCK - X_ROWS
    right_first = right_ready[:z_rows]

    def right_part(place):
        both = jnp.concatenate([columns(anchor, (1 - h) * 8 + place), columns(anchor, h * 8 + place)], axis=1)
        return dot(right_first, weights(right_pole[:BLOCK], right_z[:BLOCK], both))

    right_own = right_ready[z_rows:]
    right_wide = jnp.concatenate([right_own, x_hi_swap(right_own)], axis=1)

    def right_wide_part(place):
        return dot(right_wide, weights(right_pole, right_z, columns(anchor, h * 8 + place)))

    left_wide = jnp.concatenate([left_ready, core_swap(left_ready)], axis=1)

    def left_part(place):
        both = jnp.concatenate(
            [columns(anchor, (place * 2 + (1 - x)) * 2 + core), columns(anchor, (place * 2 + x) * 2 + core)], axis=1
        )
        return dot(left_wide, weights(left_pole, left_z, both))

    right_sum = ring(right_part, z_step, z, 8)
    right_top = right_sum[:, LANES:] + x_hi_swap(right_sum[:, :LANES].astype(jnp.bfloat16)).astype(jnp.float32)
    right_bottom = ring(right_wide_part, z_step, z, 8)
    left_sum = ring(left_part, y_step, y, 4)
    left_new = left_sum[:, LANES:] + x_lo_swap(left_sum[:, :LANES].astype(jnp.bfloat16)).astype(jnp.float32)
    right_new = jnp.concatenate([right_top, right_bottom])
    return (left_new * scale[0:1]).astype(jnp.bfloat16), (right_new * scale[1:2]).astype(jnp.bfloat16)


def solution(mesh):
    in_specs = (
        P("row", "col"),
        P("col", "row"),
        P("row", "col"),
        P("col", "row"),
        P(),
        P(),
        P(),
        P(),
        P(),
    )
    out_specs = (P("row", "col"), P("col", "row"))
    return jax.shard_map(body, mesh=mesh, in_specs=in_specs, out_specs=out_specs, check_vma=False)
```

```python
import functools

import jax
import jax.numpy as jnp
from jax import lax
from jax.experimental import pallas as pl
from jax.experimental.pallas import tpu as pltpu
from jax.sharding import PartitionSpec as P

M = 2048
TB = 512
LIVE = 12288
LANES = 128
BLOCK = 1024
N_Z = 8
N_Y = 4
F32 = jnp.float32
BF16 = jnp.bfloat16
VMEM = pl.BlockSpec(memory_space=pltpu.VMEM)
SMEM = pl.BlockSpec(memory_space=pltpu.SMEM)
HBM = pl.BlockSpec(memory_space=pltpu.HBM)
TABLE = pltpu.VMEM((6 * 64, 2 * LANES), BF16)
TALL = pltpu.VMEM((BLOCK, LANES), BF16)
PAIR = pltpu.VMEM((2 * BLOCK, LANES), BF16)


def near(x):
    return pltpu.with_memory_space_constraint(x, pltpu.VMEM)


def far(x):
    return pltpu.with_memory_space_constraint(x, pltpu.HBM)


def call(kernel, outs, deps, args, scratch=(), specs=None):
    def run(*refs):
        kernel(*refs[len(deps) :])

    specs = specs or [VMEM] * len(args)
    args = [near(a) if s is VMEM else far(a) if s is HBM else a for a, s in zip(args, specs)]
    return pl.pallas_call(
        run,
        out_shape=outs,
        in_specs=[VMEM] * len(deps) + specs,
        out_specs=VMEM if not isinstance(outs, tuple) else (VMEM,) * len(outs),
        scratch_shapes=list(scratch),
        compiler_params=pltpu.CompilerParams(vmem_limit_bytes=12 * 2**20),
        cost_estimate=pl.CostEstimate(flops=1000, bytes_accessed=1000, transcendentals=0),
    )(*(near(d) for d in deps), *args)


def split3(x):
    hi = x.astype(BF16)
    rest = x - hi.astype(F32)
    mid = rest.astype(BF16)
    low = (rest - mid.astype(F32)).astype(BF16)
    return hi, mid, low


def fill_table(table, poles_ref, zvec_ref):
    for index, ref in enumerate((poles_ref, zvec_ref)):
        for part, piece in enumerate(split3(jnp.transpose(ref[...]))):
            at = slice((3 * index + part) * 64, (3 * index + part + 1) * 64)
            table[at, :LANES] = piece[:64]
            table[at, LANES:] = piece[64:]


def pick(table, index, with_z):
    high = (index >> 7) + ((index >> 6) & 1) * LANES
    low = index & 63
    onehot = (lax.broadcasted_iota(jnp.int32, (2 * LANES, LANES), 0) == high).astype(F32).astype(BF16)
    parts = table[...] if with_z else table[: 3 * 64, :]
    got = jnp.dot(parts, onehot, preferred_element_type=F32)
    hit = lax.broadcasted_iota(jnp.int32, (64, LANES), 0) == low

    def fold(base):
        whole = got[base : base + 64] + got[base + 64 : base + 128] + got[base + 128 : base + 192]
        return jnp.sum(jnp.where(hit, whole, 0.0), axis=0, keepdims=True)

    return fold(0), (fold(192) if with_z else None)


def pick_block(table, perm_ref, block, step):
    index = perm_ref[pl.ds(block * (BLOCK // LANES) + step, 1), :]
    pole, z = pick(table, index, True)
    return pole, jnp.where(index < LIVE, z, 0.0)


def pick_anchor(table, root_ref, gaps_ref, shard):
    pole, _ = pick(table, root_ref[pl.ds(shard, 1), :], False)
    gap = gaps_ref[pl.ds(shard, 1), :]
    return jnp.concatenate([pole, gap, pole + gap, jnp.zeros((5, LANES), F32)])


def weigh(w, rows, cols, anchor):
    k, g, s = anchor[0:1], anchor[1:2], anchor[2:3]
    for step in range(rows // LANES):
        at = slice(step * LANES, (step + 1) * LANES)
        pole, z = cols[at, 0:1], cols[at, 1:2]
        denom = ((pole - k) - g) * (pole + s)
        w[at, :] = (z * pltpu.reciprocal(denom, approx=True)).astype(BF16)


def lanes_of(anchor_ref, shard):
    return anchor_ref[:, pl.ds(pl.multiple_of(shard * LANES, LANES), LANES)]


def position():
    r, q = lax.axis_index("row"), lax.axis_index("col")
    return r // N_Z, r % N_Z, q // 4, (q // 2) % 2, q % 2


def mask_into(out_ref, map_ref, in_ref):
    for i in range(BLOCK // TB):
        for j in range(BLOCK // TB):
            at = (slice(i * TB, (i + 1) * TB), slice(j * TB, (j + 1) * TB))
            keep = map_ref[i, j] != 0

            @pl.when(keep)
            def _():
                out_ref[at] = in_ref[at]

            @pl.when(jnp.logical_not(keep))
            def _():
                out_ref[at] = jnp.zeros((TB, TB), BF16)


def toward(place, size, distance):
    return lax.rem(place + size + (1 - 2 * lax.rem(place, 2)) * distance, size)


def z_shards(distance):
    h, z = position()[:2]
    place = toward(z, N_Z, distance)
    return (1 - h) * N_Z + place, h * N_Z + place


def z_chunk(right_ref, cols, both, w, other_ref, own_ref):
    weigh(w, BLOCK, cols, both)
    for half in range(2):
        at = slice(half * TB, (half + 1) * TB)
        got = jnp.dot(right_ref[at], w[...], preferred_element_type=F32)
        other_ref[at] = got[:, :LANES].astype(BF16)
        own_ref[at] = got[:, LANES:].astype(BF16)


def first_kernel(
    map_hbm, right_hbm, perm_hbm, poles_hbm, zvec_hbm, root_hbm, gaps_hbm,
    other_ref, own_ref, cols_ref, ready_ref, table,
    rows, w, raw, map_ref, perm_ref, poles_ref, zvec_ref, root_ref, gaps_ref, sems,
):
    pairs = (
        (poles_hbm, poles_ref),
        (zvec_hbm, zvec_ref),
        (perm_hbm, perm_ref),
        (root_hbm, root_ref),
        (gaps_hbm, gaps_ref),
        (map_hbm, map_ref),
        (right_hbm, raw),
    )
    copies = [pltpu.make_async_copy(a, b, sems.at[index]) for index, (a, b) in enumerate(pairs)]
    for copy in copies:
        copy.start()
    for copy in copies[:-1]:
        copy.wait()
    fill_table(table, poles_ref, zvec_ref)
    block = lax.axis_index("row")
    rows[...] = jnp.zeros_like(rows)
    for step in range(BLOCK // LANES):
        pole, z = pick_block(table, perm_ref, block, step)
        at = slice(step * LANES, (step + 1) * LANES)
        rows[0:1, at] = pole
        rows[1:2, at] = z * pole
    cols_ref[...] = jnp.transpose(rows[...])
    other, own = z_shards(N_Z // 2)
    both = [pick_anchor(table, root_ref, gaps_ref, shard) for shard in (other, own)]
    copies[-1].wait()
    mask_into(ready_ref, map_ref, raw)
    z_chunk(ready_ref, cols_ref, jnp.concatenate(both, axis=1), w, other_ref, own_ref)


def first(*args):
    square = pltpu.VMEM((LANES, LANES), F32)
    return call(
        first_kernel,
        (TALL, TALL, pltpu.VMEM((BLOCK, 8), F32), pltpu.VMEM((BLOCK, BLOCK), BF16), TABLE),
        (),
        args,
        [
            pltpu.VMEM((8, BLOCK), F32),
            pltpu.VMEM((BLOCK, 2 * LANES), BF16),
            pltpu.VMEM((BLOCK, BLOCK), BF16),
            pltpu.SMEM((2, 2), jnp.int32),
            pltpu.VMEM((LANES, LANES), jnp.int32),
            square,
            square,
            pltpu.VMEM((M // LANES, LANES), jnp.int32),
            pltpu.VMEM((M // LANES, LANES), F32),
            pltpu.SemaphoreType.DMA((7,)),
        ],
        [HBM] * 7,
    )


def mask_kernel(map_ref, in_ref, out_ref):
    mask_into(out_ref, map_ref, in_ref)


def masked(deps, tiles, block):
    return call(mask_kernel, pltpu.VMEM(block.shape, BF16), deps, (tiles, block), (), [SMEM, VMEM])


def chunk_kernel(distances, right_ref, cols_ref, anchor_ref, *refs):
    outs, ws = refs[: 2 * len(distances)], refs[2 * len(distances) :]
    for index, distance in enumerate(distances):
        both = jnp.concatenate([lanes_of(anchor_ref, shard) for shard in z_shards(distance)], axis=1)
        z_chunk(right_ref, cols_ref, both, ws[index % 2], outs[2 * index], outs[2 * index + 1])


def chunks(distances, deps, right_ready, cols, anchor):
    return call(
        functools.partial(chunk_kernel, distances),
        (TALL,) * (2 * len(distances)),
        deps,
        (right_ready, cols, anchor),
        [pltpu.VMEM((BLOCK, 2 * LANES), BF16)] * 2,
    )


def second_kernel(right_ref, cols_ref, table, root_ref, gaps_ref, anchor_ref, *refs):
    for shard in range(M // LANES):
        anchor_ref[:, shard * LANES : (shard + 1) * LANES] = pick_anchor(table, root_ref, gaps_ref, shard)
    chunk_kernel((3, -3), right_ref, cols_ref, anchor_ref, *refs)


def second(deps, *args):
    outs = (pltpu.VMEM((8, M), F32),) + (TALL,) * 4
    return call(second_kernel, outs, deps, args, [pltpu.VMEM((BLOCK, 2 * LANES), BF16)] * 2)


def left_kernel(own_ref, other_ref, table, perm_ref, anchor_ref, *refs):
    outs, (rows, cols, w0, w1) = refs[: 2 * N_Y], refs[2 * N_Y :]
    block = lax.axis_index("col")
    _, _, y, x, core = position()
    rows[...] = jnp.zeros_like(rows)
    for part in range(2):
        at_block = block if part == 0 else block + 1 - 2 * core
        for step in range(BLOCK // LANES):
            at = slice(part * BLOCK + step * LANES, part * BLOCK + (step + 1) * LANES)
            pole, z = pick_block(table, perm_ref, at_block, step)
            rows[0:1, at] = pole
            rows[1:2, at] = z
    cols[...] = jnp.transpose(rows[...])
    for index, distance in enumerate((2, 1, -1, 0)):
        other_out, own_out = outs[2 * index : 2 * index + 2]
        place = toward(y, N_Y, distance)
        w = (w0, w1)[index % 2]
        shards = ((place * 2 + (1 - x)) * 2 + core, (place * 2 + x) * 2 + core)
        weigh(w, 2 * BLOCK, cols, jnp.concatenate([lanes_of(anchor_ref, shard) for shard in shards], axis=1))
        for half in range(2):
            at = slice(half * TB, (half + 1) * TB)
            got = jnp.dot(own_ref[at], w[:BLOCK], preferred_element_type=F32)
            got += jnp.dot(other_ref[at], w[BLOCK:], preferred_element_type=F32)
            other_out[at] = got[:, :LANES].astype(BF16)
            own_out[at] = got[:, LANES:].astype(BF16)


def left_parts(deps, *args):
    scratch = [pltpu.VMEM((8, 2 * BLOCK), F32), pltpu.VMEM((2 * BLOCK, 8), F32)]
    scratch += [pltpu.VMEM((2 * BLOCK, 2 * LANES), BF16)] * 2
    return call(left_kernel, (TALL,) * (2 * N_Y), deps, args, scratch)


def norm_kernel(poles_ref, zvec_ref, anchor_ref, out_ref):
    def spread(row):
        return jnp.transpose(jnp.broadcast_to(row, (LANES, LANES)))

    for side, axis in enumerate(("col", "row")):
        mine = lanes_of(anchor_ref, lax.axis_index(axis))
        anchor, gap, both = spread(mine[0:1]), spread(mine[1:2]), spread(mine[2:3])

        def step(row, total):
            pole = poles_ref[pl.ds(row, 1), :]
            z = zvec_ref[pl.ds(row, 1), :]
            if side:
                z = z * pole
            weight = z * pltpu.reciprocal(((pole - anchor) - gap) * (pole + both), approx=True)
            return total + weight * weight

        total = lax.fori_loop(0, LIVE // LANES, step, jnp.zeros((LANES, LANES), F32))
        sums = jnp.sum(jnp.transpose(total), axis=0, keepdims=True)
        out_ref[side : side + 1, :] = 1.0 / jnp.sqrt(sums)


def norms(deps, *args):
    return call(norm_kernel, pltpu.VMEM((2, LANES), F32), deps, args)


def total(*refs):
    value = refs[0][...].astype(F32)
    for ref in refs[1:]:
        value = value + ref[...].astype(F32)
    return value.astype(BF16)


def head_kernel(moved, other, own, out):
    out[:BLOCK] = total(moved, other)
    out[BLOCK:] = own[...]


def tail_kernel(moved, other, own, out):
    out[:BLOCK] = other[...]
    out[BLOCK:] = total(moved, own)


def pair_kernel(moved, other, own, out):
    out[:BLOCK] = total(moved.at[:BLOCK], other)
    out[BLOCK:] = total(moved.at[BLOCK:], own)


def half_kernel(start, moved, part, out):
    out[...] = total(moved.at[start : start + BLOCK], part)


def sum_kernel(start, part, *refs):
    refs, out = refs[:-1], refs[-1]
    out[...] = total(part, *(ref.at[start : start + BLOCK] for ref in refs))


def swap(value, axis, partners):
    return lax.ppermute(value, axis, list(enumerate(partners)))


def z_swap(value, odd):
    partner = [(((z + odd) ^ 1) - odd) % N_Z for z in range(N_Z)]
    return swap(value, "row", [h * N_Z + partner[z] for h in range(2) for z in range(N_Z)])


def y_swap(value, odd):
    partner = [(((y + odd) ^ 1) - odd) % N_Y for y in range(N_Y)]
    return swap(value, "col", [partner[q // 4] * 4 + q % 4 for q in range(16)])


def x_hi_swap(value):
    return swap(value, "row", [(r + 8) % 16 for r in range(16)])


def x_lo_swap(value):
    return swap(value, "col", [q ^ 2 for q in range(16)])


def core_swap(value):
    return swap(value, "col", [q ^ 1 for q in range(16)])


def add(*values):
    result = values[0].astype(F32)
    for value in values[1:]:
        result = result + value.astype(F32)
    return result


def body(left_old, right_old, left_map, right_map, poles, zvec, perm, gaps, root_pole):
    poles = poles.reshape(LANES, LANES)
    zvec = zvec.reshape(LANES, LANES)
    perm = perm.reshape(LANES, LANES)
    gaps = gaps.reshape(M // LANES, LANES)
    root = root_pole.reshape(M // LANES, LANES)

    far_other, far_own, cols, right_ready, table = first(right_map, right_old, perm, poles, zvec, root, gaps)
    in_a, in_b = z_swap(far_other, 0), z_swap(far_own, 1)
    left_own = masked((far_own,), left_map, left_old)
    left_other = core_swap(left_own)
    anchor, *part = second((left_own,), right_ready, cols, table, root, gaps)
    out_b = call(head_kernel, PAIR, (), (in_a, part[2], part[3]))
    out_a = call(tail_kernel, PAIR, (out_b,), (in_b, part[0], part[1]))
    in_b, in_a = z_swap(out_b, 1), z_swap(out_a, 0)
    l_parts = left_parts((out_a,), left_own, left_other, table, perm, anchor)
    l_in_a, l_in_b = y_swap(l_parts[0], 0), y_swap(l_parts[1], 1)
    part = chunks((2, -2), (l_parts[7],), right_ready, cols, anchor)
    out_a = call(pair_kernel, PAIR, (), (in_b, part[0], part[1]))
    out_b = call(pair_kernel, PAIR, (out_a,), (in_a, part[2], part[3]))
    in_a, in_b = z_swap(out_a, 0), z_swap(out_b, 1)
    l_b = call(head_kernel, PAIR, (out_b,), (l_in_a, l_parts[4], l_parts[5]))
    l_a = call(tail_kernel, PAIR, (l_b,), (l_in_b, l_parts[2], l_parts[3]))
    l_b, l_a, l_dep = y_swap(l_b, 1), y_swap(l_a, 0), l_a
    part = chunks((1, -1, 0), (l_dep,), right_ready, cols, anchor)
    scale = norms((part[5],), poles, zvec, anchor)
    first_half, second_half = functools.partial(half_kernel, 0), functools.partial(half_kernel, BLOCK)
    out_b_other = call(first_half, TALL, (scale,), (in_a, part[2]))
    out_a_other = call(first_half, TALL, (out_b_other,), (in_b, part[0]))
    out_b_own = call(second_half, TALL, (out_a_other,), (in_a, part[3]))
    out_a_own = call(second_half, TALL, (out_b_own,), (in_b, part[1]))
    l_away = call(functools.partial(sum_kernel, 0), TALL, (out_a_own,), (l_parts[6], l_a, l_b))
    away = call(functools.partial(sum_kernel, 0), TALL, (l_away,), (part[4], z_swap(out_b_other, 1), z_swap(out_a_other, 0)))
    own = add(part[5], z_swap(out_b_own, 1), z_swap(out_a_own, 0))
    right_new = add(own, x_hi_swap(away))
    left_new = add(l_parts[7], l_a[BLOCK:], l_b[BLOCK:], x_lo_swap(l_away))
    return (left_new * scale[0:1]).astype(BF16), (right_new * scale[1:2]).astype(BF16)


def solution(mesh):
    in_specs = (
        P("row", "col"),
        P("col", "row"),
        P("row", "col"),
        P("col", "row"),
        P(),
        P(),
        P(),
        P(),
        P(),
    )
    out_specs = (P("row", "col"), P("col", "row"))
    return jax.shard_map(body, mesh=mesh, in_specs=in_specs, out_specs=out_specs, check_vma=False)
```

```python
import functools

import jax
import jax.numpy as jnp
from jax import lax
from jax.experimental import pallas as pl
from jax.experimental.pallas import tpu as pltpu
from jax.sharding import PartitionSpec as P

M = 2048
TB = 512
LIVE = 12288
LANES = 128
BLOCK = 1024
N_Z = 8
N_Y = 4
F32 = jnp.float32
BF16 = jnp.bfloat16
VMEM = pl.BlockSpec(memory_space=pltpu.VMEM)
SMEM = pl.BlockSpec(memory_space=pltpu.SMEM)
HBM = pl.BlockSpec(memory_space=pltpu.HBM)
TABLE = pltpu.VMEM((6 * 64, 2 * LANES), BF16)
TALL = pltpu.VMEM((BLOCK, LANES), BF16)
PAIR = pltpu.VMEM((2 * BLOCK, LANES), BF16)


def near(x):
    return pltpu.with_memory_space_constraint(x, pltpu.VMEM)


def far(x):
    return pltpu.with_memory_space_constraint(x, pltpu.HBM)


def call(kernel, outs, deps, args, scratch=(), specs=None):
    def run(*refs):
        kernel(*refs[len(deps) :])

    specs = specs or [VMEM] * len(args)
    args = [near(a) if s is VMEM else far(a) if s is HBM else a for a, s in zip(args, specs)]
    return pl.pallas_call(
        run,
        out_shape=outs,
        in_specs=[VMEM] * len(deps) + specs,
        out_specs=VMEM if not isinstance(outs, tuple) else (VMEM,) * len(outs),
        scratch_shapes=list(scratch),
        compiler_params=pltpu.CompilerParams(vmem_limit_bytes=12 * 2**20),
        cost_estimate=pl.CostEstimate(flops=1000, bytes_accessed=1000, transcendentals=0),
    )(*(near(d) for d in deps), *args)


def split3(x):
    hi = x.astype(BF16)
    rest = x - hi.astype(F32)
    mid = rest.astype(BF16)
    low = (rest - mid.astype(F32)).astype(BF16)
    return hi, mid, low


def fill_table(table, poles_ref, zvec_ref):
    for index, ref in enumerate((poles_ref, zvec_ref)):
        for part, piece in enumerate(split3(jnp.transpose(ref[...]))):
            at = slice((3 * index + part) * 64, (3 * index + part + 1) * 64)
            table[at, :LANES] = piece[:64]
            table[at, LANES:] = piece[64:]


def pick(table, index, with_z):
    high = (index >> 7) + ((index >> 6) & 1) * LANES
    low = index & 63
    onehot = (lax.broadcasted_iota(jnp.int32, (2 * LANES, LANES), 0) == high).astype(F32).astype(BF16)
    parts = table[...] if with_z else table[: 3 * 64, :]
    got = jnp.dot(parts, onehot, preferred_element_type=F32)
    hit = lax.broadcasted_iota(jnp.int32, (64, LANES), 0) == low

    def fold(base):
        whole = got[base : base + 64] + got[base + 64 : base + 128] + got[base + 128 : base + 192]
        return jnp.sum(jnp.where(hit, whole, 0.0), axis=0, keepdims=True)

    return fold(0), (fold(192) if with_z else None)


def pick_block(table, perm_ref, block, step):
    index = perm_ref[pl.ds(block * (BLOCK // LANES) + step, 1), :]
    pole, z = pick(table, index, True)
    return pole, jnp.where(index < LIVE, z, 0.0)


def pick_anchor(table, root_ref, gaps_ref, shard):
    pole, _ = pick(table, root_ref[pl.ds(shard, 1), :], False)
    gap = gaps_ref[pl.ds(shard, 1), :]
    return jnp.concatenate([pole, gap, pole + gap, jnp.zeros((5, LANES), F32)])


def weigh(w, rows, cols, anchor):
    k, g, s = anchor[0:1], anchor[1:2], anchor[2:3]
    for step in range(rows // LANES):
        at = slice(step * LANES, (step + 1) * LANES)
        pole, z = cols[at, 0:1], cols[at, 1:2]
        denom = ((pole - k) - g) * (pole + s)
        w[at, :] = (z * pltpu.reciprocal(denom, approx=True)).astype(BF16)


def lanes_of(anchor_ref, shard):
    return anchor_ref[:, pl.ds(pl.multiple_of(shard * LANES, LANES), LANES)]


def position():
    r, q = lax.axis_index("row"), lax.axis_index("col")
    return r // N_Z, r % N_Z, q // 4, (q // 2) % 2, q % 2


def mask_into(out_ref, map_ref, in_ref):
    for i in range(BLOCK // TB):
        for j in range(BLOCK // TB):
            at = (slice(i * TB, (i + 1) * TB), slice(j * TB, (j + 1) * TB))
            keep = map_ref[i, j] != 0

            @pl.when(keep)
            def _():
                out_ref[at] = in_ref[at]

            @pl.when(jnp.logical_not(keep))
            def _():
                out_ref[at] = jnp.zeros((TB, TB), BF16)


def toward(place, size, distance):
    return lax.rem(place + size + (1 - 2 * lax.rem(place, 2)) * distance, size)


def z_shards(distance):
    h, z = position()[:2]
    place = toward(z, N_Z, distance)
    return (1 - h) * N_Z + place, h * N_Z + place


def z_chunk(right_ref, cols, both, w, other_ref, own_ref):
    weigh(w, BLOCK, cols, both)
    for half in range(2):
        at = slice(half * TB, (half + 1) * TB)
        got = jnp.dot(right_ref[at], w[...], preferred_element_type=F32)
        other_ref[at] = got[:, :LANES].astype(BF16)
        own_ref[at] = got[:, LANES:].astype(BF16)


def first_kernel(
    left_map_hbm, left_hbm, map_hbm, right_hbm, perm_hbm, poles_hbm, zvec_hbm, root_hbm, gaps_hbm,
    other_ref, own_ref, cols_ref, ready_ref, table, left_ready_ref,
    rows, w, raw, left_raw, map_ref, left_map_ref, perm_ref, poles_ref, zvec_ref, root_ref, gaps_ref, sems,
):
    pairs = (
        (poles_hbm, poles_ref),
        (zvec_hbm, zvec_ref),
        (perm_hbm, perm_ref),
        (root_hbm, root_ref),
        (gaps_hbm, gaps_ref),
        (map_hbm, map_ref),
        (left_map_hbm, left_map_ref),
        (right_hbm, raw),
        (left_hbm, left_raw),
    )
    copies = [pltpu.make_async_copy(a, b, sems.at[index]) for index, (a, b) in enumerate(pairs)]
    for copy in copies:
        copy.start()
    for copy in copies[:-2]:
        copy.wait()
    fill_table(table, poles_ref, zvec_ref)
    block = lax.axis_index("row")
    rows[...] = jnp.zeros_like(rows)
    for step in range(BLOCK // LANES):
        pole, z = pick_block(table, perm_ref, block, step)
        at = slice(step * LANES, (step + 1) * LANES)
        rows[0:1, at] = pole
        rows[1:2, at] = z * pole
    cols_ref[...] = jnp.transpose(rows[...])
    other, own = z_shards(N_Z // 2)
    both = [pick_anchor(table, root_ref, gaps_ref, shard) for shard in (other, own)]
    copies[-2].wait()
    mask_into(ready_ref, map_ref, raw)
    z_chunk(ready_ref, cols_ref, jnp.concatenate(both, axis=1), w, other_ref, own_ref)
    copies[-1].wait()
    mask_into(left_ready_ref, left_map_ref, left_raw)


def first(*args):
    square, plane = pltpu.VMEM((BLOCK, BLOCK), BF16), pltpu.VMEM((LANES, LANES), F32)
    return call(
        first_kernel,
        (TALL, TALL, pltpu.VMEM((BLOCK, 8), F32), square, TABLE, square),
        (),
        args,
        [
            pltpu.VMEM((8, BLOCK), F32),
            pltpu.VMEM((BLOCK, 2 * LANES), BF16),
            square,
            square,
            pltpu.SMEM((2, 2), jnp.int32),
            pltpu.SMEM((2, 2), jnp.int32),
            pltpu.VMEM((LANES, LANES), jnp.int32),
            plane,
            plane,
            pltpu.VMEM((M // LANES, LANES), jnp.int32),
            pltpu.VMEM((M // LANES, LANES), F32),
            pltpu.SemaphoreType.DMA((9,)),
        ],
        [HBM] * 9,
    )


def left_lookup_kernel(table, perm_ref, cols, rows):
    block = lax.axis_index("col")
    core = position()[4]
    rows[...] = jnp.zeros_like(rows)
    for part in range(2):
        at_block = block if part == 0 else block + 1 - 2 * core
        for step in range(BLOCK // LANES):
            at = slice(part * BLOCK + step * LANES, part * BLOCK + (step + 1) * LANES)
            pole, z = pick_block(table, perm_ref, at_block, step)
            rows[0:1, at] = pole
            rows[1:2, at] = z
    cols[...] = jnp.transpose(rows[...])


def left_lookup(deps, *args):
    return call(left_lookup_kernel, pltpu.VMEM((2 * BLOCK, 8), F32), deps, args, [pltpu.VMEM((8, 2 * BLOCK), F32)])


def chunk_kernel(distances, right_ref, cols_ref, anchor_ref, *refs):
    outs, ws = refs[: 2 * len(distances)], refs[2 * len(distances) :]
    for index, distance in enumerate(distances):
        both = jnp.concatenate([lanes_of(anchor_ref, shard) for shard in z_shards(distance)], axis=1)
        z_chunk(right_ref, cols_ref, both, ws[index % 2], outs[2 * index], outs[2 * index + 1])


def chunks(distances, deps, right_ready, cols, anchor):
    return call(
        functools.partial(chunk_kernel, distances),
        (TALL,) * (2 * len(distances)),
        deps,
        (right_ready, cols, anchor),
        [pltpu.VMEM((BLOCK, 2 * LANES), BF16)] * 2,
    )


def second_kernel(right_ref, cols_ref, table, root_ref, gaps_ref, anchor_ref, *refs):
    for shard in range(M // LANES):
        anchor_ref[:, shard * LANES : (shard + 1) * LANES] = pick_anchor(table, root_ref, gaps_ref, shard)
    chunk_kernel((3, -3), right_ref, cols_ref, anchor_ref, *refs)


def second(deps, *args):
    outs = (pltpu.VMEM((8, M), F32),) + (TALL,) * 4
    return call(second_kernel, outs, deps, args, [pltpu.VMEM((BLOCK, 2 * LANES), BF16)] * 2)


def left_kernel(own_ref, other_ref, cols, anchor_ref, *refs):
    outs, (w0, w1) = refs[: 2 * N_Y], refs[2 * N_Y :]
    _, _, y, x, core = position()
    for index, distance in enumerate((2, 1, -1, 0)):
        other_out, own_out = outs[2 * index : 2 * index + 2]
        place = toward(y, N_Y, distance)
        w = (w0, w1)[index % 2]
        shards = ((place * 2 + (1 - x)) * 2 + core, (place * 2 + x) * 2 + core)
        weigh(w, 2 * BLOCK, cols, jnp.concatenate([lanes_of(anchor_ref, shard) for shard in shards], axis=1))
        for half in range(2):
            at = slice(half * TB, (half + 1) * TB)
            got = jnp.dot(own_ref[at], w[:BLOCK], preferred_element_type=F32)
            got += jnp.dot(other_ref[at], w[BLOCK:], preferred_element_type=F32)
            other_out[at] = got[:, :LANES].astype(BF16)
            own_out[at] = got[:, LANES:].astype(BF16)


def left_parts(deps, *args):
    return call(left_kernel, (TALL,) * (2 * N_Y), deps, args, [pltpu.VMEM((2 * BLOCK, 2 * LANES), BF16)] * 2)


def norm_kernel(poles_ref, zvec_ref, anchor_ref, out_ref, sums_ref):
    half = LANES // 2

    def spread(row):
        return jnp.transpose(jnp.broadcast_to(row, (LANES, LANES)))

    for side, axis in enumerate(("col", "row")):
        mine = lanes_of(anchor_ref, lax.axis_index(axis))
        columns = [spread(mine[i : i + 1]) for i in range(3)]
        for part in range(2):
            at = slice(part * half, (part + 1) * half)
            anchor, gap, both = (column[at] for column in columns)

            def step(row, total):
                pole = poles_ref[pl.ds(row, 1), :]
                z = zvec_ref[pl.ds(row, 1), :]
                if side:
                    z = z * pole
                weight = z * pltpu.reciprocal(((pole - anchor) - gap) * (pole + both), approx=True)
                return total + weight * weight

            sums_ref[at] = lax.fori_loop(0, LIVE // LANES, step, jnp.zeros((half, LANES), F32), unroll=4)
        sums = jnp.sum(jnp.transpose(sums_ref[...]), axis=0, keepdims=True)
        out_ref[side : side + 1, :] = 1.0 / jnp.sqrt(sums)


def norms(deps, *args):
    return call(norm_kernel, pltpu.VMEM((2, LANES), F32), deps, args, [pltpu.VMEM((LANES, LANES), F32)])


def total(*refs):
    value = refs[0][...].astype(F32)
    for ref in refs[1:]:
        value = value + ref[...].astype(F32)
    return value.astype(BF16)


def merge_kernel(*refs):
    refs[-1][...] = total(*refs[:-1])


def merge(deps, *values):
    return call(merge_kernel, TALL, deps, values)


def head_kernel(moved, other, own, out):
    out[:BLOCK] = total(moved, other)
    out[BLOCK:] = own[...]


def tail_kernel(moved, other, own, out):
    out[:BLOCK] = other[...]
    out[BLOCK:] = total(moved, own)


def pair_kernel(other_in, own_in, other, own, out):
    out[:BLOCK] = total(other_in, other)
    out[BLOCK:] = total(own_in, own)


def half_kernel(start, moved, part, out):
    out[...] = total(moved.at[start : start + BLOCK], part)


def sum_kernel(start, part, *refs):
    refs, out = refs[:-1], refs[-1]
    out[...] = total(part, *(ref.at[start : start + BLOCK] for ref in refs))


def swap(value, axis, partners):
    return lax.ppermute(value, axis, list(enumerate(partners)))


def z_swap(value, odd):
    partner = [(((z + odd) ^ 1) - odd) % N_Z for z in range(N_Z)]
    return swap(value, "row", [h * N_Z + partner[z] for h in range(2) for z in range(N_Z)])


def y_swap(value, odd):
    partner = [(((y + odd) ^ 1) - odd) % N_Y for y in range(N_Y)]
    return swap(value, "col", [partner[q // 4] * 4 + q % 4 for q in range(16)])


def x_hi_swap(value):
    return swap(value, "row", [(r + 8) % 16 for r in range(16)])


def x_lo_swap(value):
    return swap(value, "col", [q ^ 2 for q in range(16)])


def core_swap(value):
    return swap(value, "col", [q ^ 1 for q in range(16)])


def add(*values):
    result = values[0].astype(F32)
    for value in values[1:]:
        result = result + value.astype(F32)
    return result


def body(left_old, right_old, left_map, right_map, poles, zvec, perm, gaps, root_pole):
    poles = poles.reshape(LANES, LANES)
    zvec = zvec.reshape(LANES, LANES)
    perm = perm.reshape(LANES, LANES)
    gaps = gaps.reshape(M // LANES, LANES)
    root = root_pole.reshape(M // LANES, LANES)

    far_other, far_own, cols, right_ready, table, left_own = first(
        left_map, left_old, right_map, right_old, perm, poles, zvec, root, gaps
    )
    left_other = core_swap(left_own)
    a_o1, b_w1 = z_swap(far_other, 0), z_swap(far_own, 1)
    anchor, *part = second((), right_ready, cols, table, root, gaps)
    a_o2, b_w2 = z_swap(part[0], 0), z_swap(part[3], 1)
    near_part = chunks((2, -2), (), right_ready, cols, anchor)
    l_cols = left_lookup((near_part[0],), table, perm)
    b_o = merge((l_cols,), a_o1, part[2])
    a_w = merge((b_o,), b_w1, part[1])
    b_o2, a_w2 = z_swap(b_o, 1), z_swap(a_w, 0)
    l_parts = left_parts((a_w,), left_own, left_other, l_cols, anchor)
    l_in_a, l_in_b = y_swap(l_parts[0], 0), y_swap(l_parts[1], 1)
    out_a = call(pair_kernel, PAIR, (l_parts[7],), (b_o2, b_w2, near_part[0], near_part[1]))
    out_b = call(pair_kernel, PAIR, (out_a,), (a_o2, a_w2, near_part[2], near_part[3]))
    in_a, in_b = z_swap(out_a, 0), z_swap(out_b, 1)
    l_b = call(head_kernel, PAIR, (out_b,), (l_in_a, l_parts[4], l_parts[5]))
    l_a = call(tail_kernel, PAIR, (l_b,), (l_in_b, l_parts[2], l_parts[3]))
    l_b, l_a, l_dep = y_swap(l_b, 1), y_swap(l_a, 0), l_a
    part = chunks((1, -1, 0), (l_dep,), right_ready, cols, anchor)
    scale = norms((part[5],), poles, zvec, anchor)
    first_half, second_half = functools.partial(half_kernel, 0), functools.partial(half_kernel, BLOCK)
    out_b_other = call(first_half, TALL, (scale,), (in_a, part[2]))
    out_a_other = call(first_half, TALL, (out_b_other,), (in_b, part[0]))
    out_b_own = call(second_half, TALL, (out_a_other,), (in_a, part[3]))
    out_a_own = call(second_half, TALL, (out_b_own,), (in_b, part[1]))
    l_away = call(functools.partial(sum_kernel, 0), TALL, (out_a_own,), (l_parts[6], l_a, l_b))
    away = merge((l_away,), part[4], z_swap(out_b_other, 1), z_swap(out_a_other, 0))
    own = add(part[5], z_swap(out_b_own, 1), z_swap(out_a_own, 0))
    right_new = add(own, x_hi_swap(away))
    left_new = add(l_parts[7], l_a[BLOCK:], l_b[BLOCK:], x_lo_swap(l_away))
    return (left_new * scale[0:1]).astype(BF16), (right_new * scale[1:2]).astype(BF16)


def solution(mesh):
    in_specs = (
        P("row", "col"),
        P("col", "row"),
        P("row", "col"),
        P("col", "row"),
        P(),
        P(),
        P(),
        P(),
        P(),
    )
    out_specs = (P("row", "col"), P("col", "row"))
    return jax.shard_map(body, mesh=mesh, in_specs=in_specs, out_specs=out_specs, check_vma=False)
```

```python
import functools

import jax
import jax.numpy as jnp
from jax import lax
from jax.experimental import pallas as pl
from jax.experimental.pallas import tpu as pltpu
from jax.sharding import PartitionSpec as P

M = 2048
TB = 512
LIVE = 12288
LANES = 128
BLOCK = 1024
N_Z = 8
N_Y = 4
F32 = jnp.float32
BF16 = jnp.bfloat16
VMEM = pl.BlockSpec(memory_space=pltpu.VMEM)
SMEM = pl.BlockSpec(memory_space=pltpu.SMEM)
HBM = pl.BlockSpec(memory_space=pltpu.HBM)
TABLE = pltpu.VMEM((6 * 64, 2 * LANES), BF16)
TALL = pltpu.VMEM((BLOCK, LANES), BF16)
PAIR = pltpu.VMEM((2 * BLOCK, LANES), BF16)


def near(x):
    return pltpu.with_memory_space_constraint(x, pltpu.VMEM)


def far(x):
    return pltpu.with_memory_space_constraint(x, pltpu.HBM)


def call(kernel, outs, deps, args, scratch=(), specs=None):
    def run(*refs):
        kernel(*refs[len(deps) :])

    specs = specs or [VMEM] * len(args)
    args = [near(a) if s is VMEM else far(a) if s is HBM else a for a, s in zip(args, specs)]
    return pl.pallas_call(
        run,
        out_shape=outs,
        in_specs=[VMEM] * len(deps) + specs,
        out_specs=VMEM if not isinstance(outs, tuple) else (VMEM,) * len(outs),
        scratch_shapes=list(scratch),
        compiler_params=pltpu.CompilerParams(vmem_limit_bytes=12 * 2**20),
        cost_estimate=pl.CostEstimate(flops=1000, bytes_accessed=1000, transcendentals=0),
    )(*(near(d) for d in deps), *args)


def split3(x):
    hi = x.astype(BF16)
    rest = x - hi.astype(F32)
    mid = rest.astype(BF16)
    low = (rest - mid.astype(F32)).astype(BF16)
    return hi, mid, low


def fill_table(table, poles_ref, zvec_ref):
    for index, ref in enumerate((poles_ref, zvec_ref)):
        for part, piece in enumerate(split3(jnp.transpose(ref[...]))):
            at = slice((3 * index + part) * 64, (3 * index + part + 1) * 64)
            table[at, :LANES] = piece[:64]
            table[at, LANES:] = piece[64:]


def pick(table, index, with_z):
    high = (index >> 7) + ((index >> 6) & 1) * LANES
    low = index & 63
    onehot = (lax.broadcasted_iota(jnp.int32, (2 * LANES, LANES), 0) == high).astype(F32).astype(BF16)
    parts = table[...] if with_z else table[: 3 * 64, :]
    got = jnp.dot(parts, onehot, preferred_element_type=F32)
    hit = lax.broadcasted_iota(jnp.int32, (64, LANES), 0) == low

    def fold(base):
        whole = got[base : base + 64] + got[base + 64 : base + 128] + got[base + 128 : base + 192]
        return jnp.sum(jnp.where(hit, whole, 0.0), axis=0, keepdims=True)

    return fold(0), (fold(192) if with_z else None)


def pick_block(table, perm_ref, block, step):
    index = perm_ref[pl.ds(block * (BLOCK // LANES) + step, 1), :]
    pole, z = pick(table, index, True)
    return pole, jnp.where(index < LIVE, z, 0.0)


def pick_anchor(table, root_ref, gaps_ref, shard):
    pole, _ = pick(table, root_ref[pl.ds(shard, 1), :], False)
    gap = gaps_ref[pl.ds(shard, 1), :]
    return jnp.concatenate([pole, gap, pole + gap, jnp.zeros((5, LANES), F32)])


def weigh(w, rows, cols, anchor):
    k, g, s = anchor[0:1], anchor[1:2], anchor[2:3]
    for step in range(rows // LANES):
        at = slice(step * LANES, (step + 1) * LANES)
        pole, z = cols[at, 0:1], cols[at, 1:2]
        denom = ((pole - k) - g) * (pole + s)
        w[at, :] = (z * pltpu.reciprocal(denom, approx=True)).astype(BF16)


def lanes_of(anchor_ref, shard):
    return anchor_ref[:, pl.ds(pl.multiple_of(shard * LANES, LANES), LANES)]


def position():
    r, q = lax.axis_index("row"), lax.axis_index("col")
    return r // N_Z, r % N_Z, q // 4, (q // 2) % 2, q % 2


def mask_into(out_ref, map_ref, in_ref):
    for i in range(BLOCK // TB):
        for j in range(BLOCK // TB):
            at = (slice(i * TB, (i + 1) * TB), slice(j * TB, (j + 1) * TB))
            keep = map_ref[i, j] != 0

            @pl.when(keep)
            def _():
                out_ref[at] = in_ref[at]

            @pl.when(jnp.logical_not(keep))
            def _():
                out_ref[at] = jnp.zeros((TB, TB), BF16)


def toward(place, size, distance):
    return lax.rem(place + size + (1 - 2 * lax.rem(place, 2)) * distance, size)


def z_shards(distance):
    h, z = position()[:2]
    place = toward(z, N_Z, distance)
    return (1 - h) * N_Z + place, h * N_Z + place


def z_chunk(right_ref, cols, both, w, other_ref, own_ref):
    weigh(w, BLOCK, cols, both)
    for half in range(2):
        at = slice(half * TB, (half + 1) * TB)
        got = jnp.dot(right_ref[at], w[...], preferred_element_type=F32)
        other_ref[at] = got[:, :LANES].astype(BF16)
        own_ref[at] = got[:, LANES:].astype(BF16)


def first_kernel(
    left_map_hbm, left_hbm, map_hbm, right_hbm, perm_hbm, poles_hbm, zvec_hbm, root_hbm, gaps_hbm,
    other_ref, own_ref, cols_ref, ready_ref, table, left_ready_ref,
    rows, w, raw, left_raw, map_ref, left_map_ref, perm_ref, poles_ref, zvec_ref, root_ref, gaps_ref, sems,
):
    pairs = (
        (poles_hbm, poles_ref),
        (zvec_hbm, zvec_ref),
        (perm_hbm, perm_ref),
        (root_hbm, root_ref),
        (gaps_hbm, gaps_ref),
        (map_hbm, map_ref),
        (left_map_hbm, left_map_ref),
        (right_hbm, raw),
        (left_hbm, left_raw),
    )
    copies = [pltpu.make_async_copy(a, b, sems.at[index]) for index, (a, b) in enumerate(pairs)]
    for copy in copies:
        copy.start()
    for copy in copies[:-2]:
        copy.wait()
    fill_table(table, poles_ref, zvec_ref)
    block = lax.axis_index("row")
    rows[...] = jnp.zeros_like(rows)
    for step in range(BLOCK // LANES):
        pole, z = pick_block(table, perm_ref, block, step)
        at = slice(step * LANES, (step + 1) * LANES)
        rows[0:1, at] = pole
        rows[1:2, at] = z * pole
    cols_ref[...] = jnp.transpose(rows[...])
    other, own = z_shards(N_Z // 2)
    both = [pick_anchor(table, root_ref, gaps_ref, shard) for shard in (other, own)]
    copies[-2].wait()
    mask_into(ready_ref, map_ref, raw)
    z_chunk(ready_ref, cols_ref, jnp.concatenate(both, axis=1), w, other_ref, own_ref)
    copies[-1].wait()
    mask_into(left_ready_ref, left_map_ref, left_raw)


def first(*args):
    square, plane = pltpu.VMEM((BLOCK, BLOCK), BF16), pltpu.VMEM((LANES, LANES), F32)
    return call(
        first_kernel,
        (TALL, TALL, pltpu.VMEM((BLOCK, 8), F32), square, TABLE, square),
        (),
        args,
        [
            pltpu.VMEM((8, BLOCK), F32),
            pltpu.VMEM((BLOCK, 2 * LANES), BF16),
            square,
            square,
            pltpu.SMEM((2, 2), jnp.int32),
            pltpu.SMEM((2, 2), jnp.int32),
            pltpu.VMEM((LANES, LANES), jnp.int32),
            plane,
            plane,
            pltpu.VMEM((M // LANES, LANES), jnp.int32),
            pltpu.VMEM((M // LANES, LANES), F32),
            pltpu.SemaphoreType.DMA((9,)),
        ],
        [HBM] * 9,
    )


def left_lookup_kernel(table, perm_ref, cols, rows):
    block = lax.axis_index("col")
    core = position()[4]
    rows[...] = jnp.zeros_like(rows)
    for part in range(2):
        at_block = block if part == 0 else block + 1 - 2 * core
        for step in range(BLOCK // LANES):
            at = slice(part * BLOCK + step * LANES, part * BLOCK + (step + 1) * LANES)
            pole, z = pick_block(table, perm_ref, at_block, step)
            rows[0:1, at] = pole
            rows[1:2, at] = z
    cols[...] = jnp.transpose(rows[...])


def left_lookup(deps, *args):
    return call(left_lookup_kernel, pltpu.VMEM((2 * BLOCK, 8), F32), deps, args, [pltpu.VMEM((8, 2 * BLOCK), F32)])


def chunk_kernel(distances, right_ref, cols_ref, anchor_ref, *refs):
    outs, ws = refs[: 2 * len(distances)], refs[2 * len(distances) :]
    for index, distance in enumerate(distances):
        both = jnp.concatenate([lanes_of(anchor_ref, shard) for shard in z_shards(distance)], axis=1)
        z_chunk(right_ref, cols_ref, both, ws[index % 2], outs[2 * index], outs[2 * index + 1])


def chunks(distances, deps, right_ready, cols, anchor):
    return call(
        functools.partial(chunk_kernel, distances),
        (TALL,) * (2 * len(distances)),
        deps,
        (right_ready, cols, anchor),
        [pltpu.VMEM((BLOCK, 2 * LANES), BF16)] * 2,
    )


def second_kernel(right_ref, cols_ref, table, root_ref, gaps_ref, anchor_ref, *refs):
    for shard in range(M // LANES):
        anchor_ref[:, shard * LANES : (shard + 1) * LANES] = pick_anchor(table, root_ref, gaps_ref, shard)
    chunk_kernel((3, -3), right_ref, cols_ref, anchor_ref, *refs)


def second(deps, *args):
    outs = (pltpu.VMEM((8, M), F32),) + (TALL,) * 4
    return call(second_kernel, outs, deps, args, [pltpu.VMEM((BLOCK, 2 * LANES), BF16)] * 2)


def left_kernel(own_ref, other_ref, cols, anchor_ref, *refs):
    outs, (w0, w1) = refs[: 2 * N_Y], refs[2 * N_Y :]
    _, _, y, x, core = position()
    for index, distance in enumerate((2, 1, -1, 0)):
        other_out, own_out = outs[2 * index : 2 * index + 2]
        place = toward(y, N_Y, distance)
        w = (w0, w1)[index % 2]
        shards = ((place * 2 + (1 - x)) * 2 + core, (place * 2 + x) * 2 + core)
        weigh(w, 2 * BLOCK, cols, jnp.concatenate([lanes_of(anchor_ref, shard) for shard in shards], axis=1))
        for half in range(2):
            at = slice(half * TB, (half + 1) * TB)
            got = jnp.dot(own_ref[at], w[:BLOCK], preferred_element_type=F32)
            got += jnp.dot(other_ref[at], w[BLOCK:], preferred_element_type=F32)
            other_out[at] = got[:, :LANES].astype(BF16)
            own_out[at] = got[:, LANES:].astype(BF16)


def left_parts(deps, *args):
    return call(left_kernel, (TALL,) * (2 * N_Y), deps, args, [pltpu.VMEM((2 * BLOCK, 2 * LANES), BF16)] * 2)


def norm_kernel(poles_ref, zvec_ref, anchor_ref, out_ref, sums_ref):
    half = LANES // 2

    def spread(row):
        return jnp.transpose(jnp.broadcast_to(row, (LANES, LANES)))

    for side, axis in enumerate(("col", "row")):
        mine = lanes_of(anchor_ref, lax.axis_index(axis))
        columns = [spread(mine[i : i + 1]) for i in range(3)]
        for part in range(2):
            at = slice(part * half, (part + 1) * half)
            anchor, gap, both = (column[at] for column in columns)

            def step(row, total):
                pole = poles_ref[pl.ds(row, 1), :]
                z = zvec_ref[pl.ds(row, 1), :]
                if side:
                    z = z * pole
                weight = z * pltpu.reciprocal(((pole - anchor) - gap) * (pole + both), approx=True)
                return total + weight * weight

            sums_ref[at] = lax.fori_loop(0, LIVE // LANES, step, jnp.zeros((half, LANES), F32), unroll=4)
        sums = jnp.sum(jnp.transpose(sums_ref[...]), axis=0, keepdims=True)
        out_ref[side : side + 1, :] = 1.0 / jnp.sqrt(sums)


def norms(deps, *args):
    return call(norm_kernel, pltpu.VMEM((2, LANES), F32), deps, args, [pltpu.VMEM((LANES, LANES), F32)])


def total(*refs):
    value = refs[0][...].astype(F32)
    for ref in refs[1:]:
        value = value + ref[...].astype(F32)
    return value.astype(BF16)


def merge_kernel(*refs):
    refs[-1][...] = total(*refs[:-1])


def merge(deps, *values):
    return call(merge_kernel, TALL, deps, values)


def head_kernel(moved, other, own, out):
    out[:BLOCK] = total(moved, other)
    out[BLOCK:] = own[...]


def tail_kernel(moved, other, own, out):
    out[:BLOCK] = other[...]
    out[BLOCK:] = total(moved, own)


def pair_kernel(other_in, own_in, other, own, out):
    out[:BLOCK] = total(other_in, other)
    out[BLOCK:] = total(own_in, own)


def half_kernel(start, moved, part, out):
    out[...] = total(moved.at[start : start + BLOCK], part)


def sum_kernel(start, part, *refs):
    refs, out = refs[:-1], refs[-1]
    out[...] = total(part, *(ref.at[start : start + BLOCK] for ref in refs))


def swap(value, axis, partners):
    return lax.ppermute(value, axis, list(enumerate(partners)))


def z_swap(value, odd):
    partner = [(((z + odd) ^ 1) - odd) % N_Z for z in range(N_Z)]
    return swap(value, "row", [h * N_Z + partner[z] for h in range(2) for z in range(N_Z)])


def y_swap(value, odd):
    partner = [(((y + odd) ^ 1) - odd) % N_Y for y in range(N_Y)]
    return swap(value, "col", [partner[q // 4] * 4 + q % 4 for q in range(16)])


def x_hi_swap(value):
    return swap(value, "row", [(r + 8) % 16 for r in range(16)])


def x_lo_swap(value):
    return swap(value, "col", [q ^ 2 for q in range(16)])


def core_swap(value):
    return swap(value, "col", [q ^ 1 for q in range(16)])


def add(*values):
    result = values[0].astype(F32)
    for value in values[1:]:
        result = result + value.astype(F32)
    return result


def body(left_old, right_old, left_map, right_map, poles, zvec, perm, gaps, root_pole):
    poles = poles.reshape(LANES, LANES)
    zvec = zvec.reshape(LANES, LANES)
    perm = perm.reshape(LANES, LANES)
    gaps = gaps.reshape(M // LANES, LANES)
    root = root_pole.reshape(M // LANES, LANES)

    far_other, far_own, cols, right_ready, table, left_own = first(
        left_map, left_old, right_map, right_old, perm, poles, zvec, root, gaps
    )
    left_other = core_swap(left_own)
    a_o1, b_w1 = z_swap(far_other, 0), z_swap(far_own, 1)
    anchor, *part = second((), right_ready, cols, table, root, gaps)
    a_o2, b_w2 = z_swap(part[0], 0), z_swap(part[3], 1)
    near_part = chunks((2, -2), (), right_ready, cols, anchor)
    l_cols = left_lookup((near_part[0],), table, perm)
    b_o = merge((l_cols,), a_o1, part[2])
    a_w = merge((b_o,), b_w1, part[1])
    b_o2, a_w2 = z_swap(b_o, 1), z_swap(a_w, 0)
    l_parts = left_parts((a_w,), left_own, left_other, l_cols, anchor)
    l_in_a, l_in_b = y_swap(l_parts[0], 0), y_swap(l_parts[1], 1)
    b_o = merge((l_parts[7],), a_o2, near_part[2])
    out_a = call(pair_kernel, PAIR, (b_o,), (b_o2, b_w2, near_part[0], near_part[1]))
    out_b = call(tail_kernel, PAIR, (out_a,), (a_w2, b_o, near_part[3]))
    in_a, in_b = z_swap(out_a, 0), z_swap(out_b, 1)
    l_b = call(head_kernel, PAIR, (out_b,), (l_in_a, l_parts[4], l_parts[5]))
    l_a = call(tail_kernel, PAIR, (l_b,), (l_in_b, l_parts[2], l_parts[3]))
    l_b, l_a, l_dep = y_swap(l_b, 1), y_swap(l_a, 0), l_a
    part = chunks((1, -1, 0), (l_dep,), right_ready, cols, anchor)
    scale = norms((part[5],), poles, zvec, anchor)
    first_half, second_half = functools.partial(half_kernel, 0), functools.partial(half_kernel, BLOCK)
    out_b_other = call(first_half, TALL, (scale,), (in_a, part[2]))
    out_a_other = call(first_half, TALL, (out_b_other,), (in_b, part[0]))
    out_b_own = call(second_half, TALL, (out_a_other,), (in_a, part[3]))
    out_a_own = call(second_half, TALL, (out_b_own,), (in_b, part[1]))
    l_away = call(functools.partial(sum_kernel, 0), TALL, (out_a_own,), (l_parts[6], l_a, l_b))
    away = merge((l_away,), part[4], z_swap(out_b_other, 1), z_swap(out_a_other, 0))
    own = add(part[5], z_swap(out_b_own, 1), z_swap(out_a_own, 0))
    right_new = add(own, x_hi_swap(away))
    left_new = add(l_parts[7], l_a[BLOCK:], l_b[BLOCK:], x_lo_swap(l_away))
    return (left_new * scale[0:1]).astype(BF16), (right_new * scale[1:2]).astype(BF16)


def solution(mesh):
    in_specs = (
        P("row", "col"),
        P("col", "row"),
        P("row", "col"),
        P("col", "row"),
        P(),
        P(),
        P(),
        P(),
        P(),
    )
    out_specs = (P("row", "col"), P("col", "row"))
    return jax.shard_map(body, mesh=mesh, in_specs=in_specs, out_specs=out_specs, check_vma=False)
```

```python
import functools

import jax
import jax.numpy as jnp
from jax import lax
from jax.experimental import pallas as pl
from jax.experimental.pallas import tpu as pltpu
from jax.sharding import PartitionSpec as P

M = 2048
TB = 512
LIVE = 12288
LANES = 128
BLOCK = 1024
N_Z = 8
N_Y = 4
F32 = jnp.float32
BF16 = jnp.bfloat16
VMEM = pl.BlockSpec(memory_space=pltpu.VMEM)
SMEM = pl.BlockSpec(memory_space=pltpu.SMEM)
HBM = pl.BlockSpec(memory_space=pltpu.HBM)
TABLE = pltpu.VMEM((6 * 64, 2 * LANES), BF16)
TALL = pltpu.VMEM((BLOCK, LANES), BF16)
PAIR = pltpu.VMEM((2 * BLOCK, LANES), BF16)


def near(x):
    return pltpu.with_memory_space_constraint(x, pltpu.VMEM)


def far(x):
    return pltpu.with_memory_space_constraint(x, pltpu.HBM)


def call(kernel, outs, deps, args, scratch=(), specs=None):
    def run(*refs):
        kernel(*refs[len(deps) :])

    specs = specs or [VMEM] * len(args)
    args = [near(a) if s is VMEM else far(a) if s is HBM else a for a, s in zip(args, specs)]
    return pl.pallas_call(
        run,
        out_shape=outs,
        in_specs=[VMEM] * len(deps) + specs,
        out_specs=VMEM if not isinstance(outs, tuple) else (VMEM,) * len(outs),
        scratch_shapes=list(scratch),
        compiler_params=pltpu.CompilerParams(vmem_limit_bytes=12 * 2**20),
        cost_estimate=pl.CostEstimate(flops=1000, bytes_accessed=1000, transcendentals=0),
    )(*(near(d) for d in deps), *args)


def split3(x):
    hi = x.astype(BF16)
    rest = x - hi.astype(F32)
    mid = rest.astype(BF16)
    low = (rest - mid.astype(F32)).astype(BF16)
    return hi, mid, low


def fill_table(table, poles_ref, zvec_ref):
    for index, ref in enumerate((poles_ref, zvec_ref)):
        for part, piece in enumerate(split3(jnp.transpose(ref[...]))):
            at = slice((3 * index + part) * 64, (3 * index + part + 1) * 64)
            table[at, :LANES] = piece[:64]
            table[at, LANES:] = piece[64:]


def pick(table, index, with_z):
    high = (index >> 7) + ((index >> 6) & 1) * LANES
    low = index & 63
    onehot = (lax.broadcasted_iota(jnp.int32, (2 * LANES, LANES), 0) == high).astype(F32).astype(BF16)
    parts = table[...] if with_z else table[: 3 * 64, :]
    got = jnp.dot(parts, onehot, preferred_element_type=F32)
    hit = lax.broadcasted_iota(jnp.int32, (64, LANES), 0) == low

    def fold(base):
        whole = got[base : base + 64] + got[base + 64 : base + 128] + got[base + 128 : base + 192]
        return jnp.sum(jnp.where(hit, whole, 0.0), axis=0, keepdims=True)

    return fold(0), (fold(192) if with_z else None)


def pick_block(table, perm_ref, block, step):
    index = perm_ref[pl.ds(block * (BLOCK // LANES) + step, 1), :]
    pole, z = pick(table, index, True)
    return pole, jnp.where(index < LIVE, z, 0.0)


def pick_anchor(table, root_ref, gaps_ref, shard):
    pole, _ = pick(table, root_ref[pl.ds(shard, 1), :], False)
    gap = gaps_ref[pl.ds(shard, 1), :]
    return jnp.concatenate([pole, gap, pole + gap, jnp.zeros((5, LANES), F32)])


def weigh(w, rows, cols, anchor):
    k, g, s = anchor[0:1], anchor[1:2], anchor[2:3]
    for step in range(rows // LANES):
        at = slice(step * LANES, (step + 1) * LANES)
        pole, z = cols[at, 0:1], cols[at, 1:2]
        denom = ((pole - k) - g) * (pole + s)
        w[at, :] = (z * pltpu.reciprocal(denom, approx=True)).astype(BF16)


def lanes_of(anchor_ref, shard):
    return anchor_ref[:, pl.ds(pl.multiple_of(shard * LANES, LANES), LANES)]


def position():
    r, q = lax.axis_index("row"), lax.axis_index("col")
    return r // N_Z, r % N_Z, q // 4, (q // 2) % 2, q % 2


def mask_into(out_ref, map_ref, in_ref):
    for i in range(BLOCK // TB):
        for j in range(BLOCK // TB):
            at = (slice(i * TB, (i + 1) * TB), slice(j * TB, (j + 1) * TB))
            keep = map_ref[i, j] != 0

            @pl.when(keep)
            def _():
                out_ref[at] = in_ref[at]

            @pl.when(jnp.logical_not(keep))
            def _():
                out_ref[at] = jnp.zeros((TB, TB), BF16)


def toward(place, size, distance):
    return lax.rem(place + size + (1 - 2 * lax.rem(place, 2)) * distance, size)


def z_shards(distance):
    h, z = position()[:2]
    place = toward(z, N_Z, distance)
    return (1 - h) * N_Z + place, h * N_Z + place


def z_chunk(right_ref, cols, both, w, other_ref, own_ref):
    weigh(w, BLOCK, cols, both)
    for half in range(2):
        at = slice(half * TB, (half + 1) * TB)
        got = jnp.dot(right_ref[at], w[...], preferred_element_type=F32)
        other_ref[at] = got[:, :LANES].astype(BF16)
        own_ref[at] = got[:, LANES:].astype(BF16)


def first_kernel(
    left_map_hbm, left_hbm, map_hbm, right_hbm, perm_hbm, poles_hbm, zvec_hbm, root_hbm, gaps_hbm,
    other_ref, own_ref, cols_ref, raw, table, left_ready_ref,
    rows, w, left_raw, map_ref, left_map_ref, perm_ref, poles_ref, zvec_ref, root_ref, gaps_ref, sems,
):
    pairs = (
        (poles_hbm, poles_ref),
        (zvec_hbm, zvec_ref),
        (perm_hbm, perm_ref),
        (root_hbm, root_ref),
        (gaps_hbm, gaps_ref),
        (map_hbm, map_ref),
        (left_map_hbm, left_map_ref),
        (right_hbm, raw),
        (left_hbm, left_raw),
    )
    copies = [pltpu.make_async_copy(a, b, sems.at[index]) for index, (a, b) in enumerate(pairs)]
    for copy in copies:
        copy.start()
    for copy in copies[:-2]:
        copy.wait()
    fill_table(table, poles_ref, zvec_ref)
    block = lax.axis_index("row")
    rows[...] = jnp.zeros_like(rows)
    for step in range(BLOCK // LANES):
        pole, z = pick_block(table, perm_ref, block, step)
        at = slice(step * LANES, (step + 1) * LANES)
        rows[0:1, at] = pole
        rows[1:2, at] = z * pole
    cols_ref[...] = jnp.transpose(rows[...])
    other, own = z_shards(N_Z // 2)
    both = [pick_anchor(table, root_ref, gaps_ref, shard) for shard in (other, own)]
    weigh(w, BLOCK, cols_ref, jnp.concatenate(both, axis=1))
    copies[-2].wait()
    for i in range(BLOCK // TB):
        at = slice(i * TB, (i + 1) * TB)
        got = jnp.zeros((TB, 2 * LANES), F32)
        for j in range(BLOCK // TB):
            across = slice(j * TB, (j + 1) * TB)
            part = jnp.dot(raw[at, across], w[across], preferred_element_type=F32)
            got += jnp.where(map_ref[i, j] != 0, part, 0.0)
        other_ref[at] = got[:, :LANES].astype(BF16)
        own_ref[at] = got[:, LANES:].astype(BF16)
    copies[-1].wait()
    mask_into(left_ready_ref, left_map_ref, left_raw)


def first(*args):
    square, plane = pltpu.VMEM((BLOCK, BLOCK), BF16), pltpu.VMEM((LANES, LANES), F32)
    return call(
        first_kernel,
        (TALL, TALL, pltpu.VMEM((BLOCK, 8), F32), square, TABLE, square),
        (),
        args,
        [
            pltpu.VMEM((8, BLOCK), F32),
            pltpu.VMEM((BLOCK, 2 * LANES), BF16),
            square,
            pltpu.SMEM((2, 2), jnp.int32),
            pltpu.SMEM((2, 2), jnp.int32),
            pltpu.VMEM((LANES, LANES), jnp.int32),
            plane,
            plane,
            pltpu.VMEM((M // LANES, LANES), jnp.int32),
            pltpu.VMEM((M // LANES, LANES), F32),
            pltpu.SemaphoreType.DMA((9,)),
        ],
        [HBM] * 9,
    )


def left_lookup_kernel(table, perm_ref, cols, rows):
    block = lax.axis_index("col")
    core = position()[4]
    rows[...] = jnp.zeros_like(rows)
    for part in range(2):
        at_block = block if part == 0 else block + 1 - 2 * core
        for step in range(BLOCK // LANES):
            at = slice(part * BLOCK + step * LANES, part * BLOCK + (step + 1) * LANES)
            pole, z = pick_block(table, perm_ref, at_block, step)
            rows[0:1, at] = pole
            rows[1:2, at] = z
    cols[...] = jnp.transpose(rows[...])


def left_lookup(deps, *args):
    return call(left_lookup_kernel, pltpu.VMEM((2 * BLOCK, 8), F32), deps, args, [pltpu.VMEM((8, 2 * BLOCK), F32)])


def chunk_kernel(distances, right_ref, cols_ref, anchor_ref, *refs):
    outs, ws = refs[: 2 * len(distances)], refs[2 * len(distances) :]
    for index, distance in enumerate(distances):
        both = jnp.concatenate([lanes_of(anchor_ref, shard) for shard in z_shards(distance)], axis=1)
        z_chunk(right_ref, cols_ref, both, ws[index % 2], outs[2 * index], outs[2 * index + 1])


def chunks(distances, deps, right_ready, cols, anchor):
    return call(
        functools.partial(chunk_kernel, distances),
        (TALL,) * (2 * len(distances)),
        deps,
        (right_ready, cols, anchor),
        [pltpu.VMEM((BLOCK, 2 * LANES), BF16)] * 2,
    )


def second_kernel(map_ref, raw, cols_ref, table, root_ref, gaps_ref, right_ref, anchor_ref, *refs):
    mask_into(right_ref, map_ref, raw)
    for shard in range(M // LANES):
        anchor_ref[:, shard * LANES : (shard + 1) * LANES] = pick_anchor(table, root_ref, gaps_ref, shard)
    chunk_kernel((3, -3), right_ref, cols_ref, anchor_ref, *refs)


def second(deps, *args):
    outs = (pltpu.VMEM((BLOCK, BLOCK), BF16), pltpu.VMEM((8, M), F32)) + (TALL,) * 4
    scratch = [pltpu.VMEM((BLOCK, 2 * LANES), BF16)] * 2
    return call(second_kernel, outs, deps, args, scratch, [SMEM] + [VMEM] * 5)


def left_kernel(own_ref, other_ref, cols, anchor_ref, *refs):
    outs, (w0, w1) = refs[: 2 * N_Y], refs[2 * N_Y :]
    _, _, y, x, core = position()
    for index, distance in enumerate((2, 1, -1, 0)):
        other_out, own_out = outs[2 * index : 2 * index + 2]
        place = toward(y, N_Y, distance)
        w = (w0, w1)[index % 2]
        shards = ((place * 2 + (1 - x)) * 2 + core, (place * 2 + x) * 2 + core)
        weigh(w, 2 * BLOCK, cols, jnp.concatenate([lanes_of(anchor_ref, shard) for shard in shards], axis=1))
        for half in range(2):
            at = slice(half * TB, (half + 1) * TB)
            got = jnp.dot(own_ref[at], w[:BLOCK], preferred_element_type=F32)
            got += jnp.dot(other_ref[at], w[BLOCK:], preferred_element_type=F32)
            other_out[at] = got[:, :LANES].astype(BF16)
            own_out[at] = got[:, LANES:].astype(BF16)


def left_parts(deps, *args):
    return call(left_kernel, (TALL,) * (2 * N_Y), deps, args, [pltpu.VMEM((2 * BLOCK, 2 * LANES), BF16)] * 2)


def norm_kernel(poles_ref, zvec_ref, anchor_ref, out_ref, sums_ref):
    half = LANES // 2

    def spread(row):
        return jnp.transpose(jnp.broadcast_to(row, (LANES, LANES)))

    for side, axis in enumerate(("col", "row")):
        mine = lanes_of(anchor_ref, lax.axis_index(axis))
        columns = [spread(mine[i : i + 1]) for i in range(3)]
        for part in range(2):
            at = slice(part * half, (part + 1) * half)
            anchor, gap, both = (column[at] for column in columns)

            def step(row, total):
                pole = poles_ref[pl.ds(row, 1), :]
                z = zvec_ref[pl.ds(row, 1), :]
                if side:
                    z = z * pole
                weight = z * pltpu.reciprocal(((pole - anchor) - gap) * (pole + both), approx=True)
                return total + weight * weight

            sums_ref[at] = lax.fori_loop(0, LIVE // LANES, step, jnp.zeros((half, LANES), F32), unroll=4)
        sums = jnp.sum(jnp.transpose(sums_ref[...]), axis=0, keepdims=True)
        out_ref[side : side + 1, :] = 1.0 / jnp.sqrt(sums)


def norms(deps, *args):
    return call(norm_kernel, pltpu.VMEM((2, LANES), F32), deps, args, [pltpu.VMEM((LANES, LANES), F32)])


def total(*refs):
    value = refs[0][...].astype(F32)
    for ref in refs[1:]:
        value = value + ref[...].astype(F32)
    return value.astype(BF16)


def merge_kernel(*refs):
    refs[-1][...] = total(*refs[:-1])


def merge(deps, *values):
    return call(merge_kernel, TALL, deps, values)


def head_kernel(moved, other, own, out):
    out[:BLOCK] = total(moved, other)
    out[BLOCK:] = own[...]


def tail_kernel(moved, other, own, out):
    out[:BLOCK] = other[...]
    out[BLOCK:] = total(moved, own)


def pair_kernel(other_in, own_in, other, own, out):
    out[:BLOCK] = total(other_in, other)
    out[BLOCK:] = total(own_in, own)


def half_kernel(start, moved, part, out):
    out[...] = total(moved.at[start : start + BLOCK], part)


def sum_kernel(start, part, *refs):
    refs, out = refs[:-1], refs[-1]
    out[...] = total(part, *(ref.at[start : start + BLOCK] for ref in refs))


def swap(value, axis, partners):
    return lax.ppermute(value, axis, list(enumerate(partners)))


def z_swap(value, odd):
    partner = [(((z + odd) ^ 1) - odd) % N_Z for z in range(N_Z)]
    return swap(value, "row", [h * N_Z + partner[z] for h in range(2) for z in range(N_Z)])


def y_swap(value, odd):
    partner = [(((y + odd) ^ 1) - odd) % N_Y for y in range(N_Y)]
    return swap(value, "col", [partner[q // 4] * 4 + q % 4 for q in range(16)])


def x_hi_swap(value):
    return swap(value, "row", [(r + 8) % 16 for r in range(16)])


def x_lo_swap(value):
    return swap(value, "col", [q ^ 2 for q in range(16)])


def core_swap(value):
    return swap(value, "col", [q ^ 1 for q in range(16)])


def add(*values):
    result = values[0].astype(F32)
    for value in values[1:]:
        result = result + value.astype(F32)
    return result


def body(left_old, right_old, left_map, right_map, poles, zvec, perm, gaps, root_pole):
    poles = poles.reshape(LANES, LANES)
    zvec = zvec.reshape(LANES, LANES)
    perm = perm.reshape(LANES, LANES)
    gaps = gaps.reshape(M // LANES, LANES)
    root = root_pole.reshape(M // LANES, LANES)

    far_other, far_own, cols, right_raw, table, left_own = first(
        left_map, left_old, right_map, right_old, perm, poles, zvec, root, gaps
    )
    left_other = core_swap(left_own)
    a_o1, b_w1 = z_swap(far_other, 0), z_swap(far_own, 1)
    right_ready, anchor, *part = second((), right_map, right_raw, cols, table, root, gaps)
    a_o2, b_w2 = z_swap(part[0], 0), z_swap(part[3], 1)
    near_part = chunks((2, -2), (), right_ready, cols, anchor)
    l_cols = left_lookup((near_part[0],), table, perm)
    b_o = merge((l_cols,), a_o1, part[2])
    a_w = merge((b_o,), b_w1, part[1])
    b_o2, a_w2 = z_swap(b_o, 1), z_swap(a_w, 0)
    l_parts = left_parts((a_w,), left_own, left_other, l_cols, anchor)
    l_in_a, l_in_b = y_swap(l_parts[0], 0), y_swap(l_parts[1], 1)
    b_o = merge((l_parts[7],), a_o2, near_part[2])
    out_a = call(pair_kernel, PAIR, (b_o,), (b_o2, b_w2, near_part[0], near_part[1]))
    out_b = call(tail_kernel, PAIR, (out_a,), (a_w2, b_o, near_part[3]))
    in_a, in_b = z_swap(out_a, 0), z_swap(out_b, 1)
    l_b = call(head_kernel, PAIR, (out_b,), (l_in_a, l_parts[4], l_parts[5]))
    l_a = call(tail_kernel, PAIR, (l_b,), (l_in_b, l_parts[2], l_parts[3]))
    l_b, l_a, l_dep = y_swap(l_b, 1), y_swap(l_a, 0), l_a
    part = chunks((1, -1, 0), (l_dep,), right_ready, cols, anchor)
    scale = norms((part[5],), poles, zvec, anchor)
    first_half, second_half = functools.partial(half_kernel, 0), functools.partial(half_kernel, BLOCK)
    out_b_other = call(first_half, TALL, (scale,), (in_a, part[2]))
    out_a_other = call(first_half, TALL, (out_b_other,), (in_b, part[0]))
    out_b_own = call(second_half, TALL, (out_a_other,), (in_a, part[3]))
    out_a_own = call(second_half, TALL, (out_b_own,), (in_b, part[1]))
    l_away = call(functools.partial(sum_kernel, 0), TALL, (out_a_own,), (l_parts[6], l_a, l_b))
    away = merge((l_away,), part[4], z_swap(out_b_other, 1), z_swap(out_a_other, 0))
    own = add(part[5], z_swap(out_b_own, 1), z_swap(out_a_own, 0))
    right_new = add(own, x_hi_swap(away))
    left_new = add(l_parts[7], l_a[BLOCK:], l_b[BLOCK:], x_lo_swap(l_away))
    return (left_new * scale[0:1]).astype(BF16), (right_new * scale[1:2]).astype(BF16)


def solution(mesh):
    in_specs = (
        P("row", "col"),
        P("col", "row"),
        P("row", "col"),
        P("col", "row"),
        P(),
        P(),
        P(),
        P(),
        P(),
    )
    out_specs = (P("row", "col"), P("col", "row"))
    return jax.shard_map(body, mesh=mesh, in_specs=in_specs, out_specs=out_specs, check_vma=False)
```
